32 devices in a mesh: blk: 16 (over z, y, core), uly: 2 (over x).
Axes of the slice: x: 2, y: 2, z: 4, core: 2. Of those that a mesh axis runs over, the one named last changes fastest.
Arguments:
- queries: bfloat16 [1024, 3072], P(('blk', 'uly')), may hold values from -40 to 40
- keys: bfloat16 [1024, 3072], P(('blk', 'uly')), may hold values from -6 to 6
- values: bfloat16 [1024, 3072], P(('blk', 'uly')), may hold values from -6 to 6
Outputs:
- attended: bfloat16 [1024, 3072], P(('blk', 'uly'))
The draws below stay inside these ranges and needn't reach their ends.
All inputs are finite; a program needn't handle non-finite values.
Results may differ from the reference program's by a relative error of at most 0.0035.
Values may be sent and summed in bfloat16 or wider, within the bound.
No kernel may reach another device: no remote copies, remote signals or barrier semaphores. Data moves between devices by JAX's collectives and lax.ppermute only.
A program may use at most 128 MiB of HBM per device.

```python
import math
import jax
import jax.numpy as jnp
from jax import lax

HEADS = 24
DIM = 3072
TOKENS = 1024


def shared_normal(key):
    return jax.random.normal(key, (TOKENS, DIM), jnp.float32)


def draw_keys(key, part):
    source_normal = shared_normal(key)
    result = jnp.clip(source_normal, -6.0, 6.0)
    return result.astype(jnp.bfloat16)


def draw_queries(key, part):
    key = jax.random.fold_in(key, 23)
    result = 2.5 * jnp.clip(jax.random.normal(key, (TOKENS, DIM), jnp.float32), -6.0, 6.0)
    return result.astype(jnp.bfloat16)


def steps_of(stream_key, shape, split, least, top_value):
    gain, own = 1.0, jax.random.fold_in(stream_key, 6)
    for axis_at, blocks in split:
        steps = jnp.exp(jax.random.uniform(jax.random.fold_in(own, axis_at), (blocks,), jnp.float32, least / len(split), top_value / len(split)))
        gain = gain * jnp.repeat(steps, shape[axis_at] // blocks).reshape([-1 if axis == axis_at else 1 for axis in range(len(shape))])
    return gain


def bell_draw(key, extent, spread, bound, shards=(), held_as=jnp.bfloat16):
    drawn = jax.random.normal(key, extent, jnp.float32) * spread
    if len(shards) > 0:
        drawn = steps_of(key, extent, shards, -0.22, 0.18) * drawn
    return jnp.clip(drawn, min=-bound, max=bound).astype(held_as)


def setup_inputs(seed: int = 0) -> dict:
    key_of = jax.random.split(jax.random.key(seed), 4)
    return {
        "queries": draw_queries(jax.random.fold_in(key_of[3], 71), 0),
        "keys": draw_keys(jax.random.fold_in(key_of[3], 71), 0),
        "values": bell_draw(key_of[2], (TOKENS, DIM), 1.0, 6.0, ((0, 32),)),
    }


def reference(queries, keys, values):
    head_width = DIM // HEADS
    score_scale = 1.0 / math.sqrt(head_width)

    def split_heads(matrix):
        return matrix.reshape(TOKENS, HEADS, head_width).transpose(1, 0, 2)

    def one_head(triple):
        query_head, key_head, value_head = triple
        scores = jnp.dot(query_head, key_head.T, preferred_element_type=jnp.float32) * score_scale
        highest = lax.optimization_barrier(jnp.max(scores, axis=1, keepdims=True))
        weights = jnp.exp(scores - highest)
        denominator = lax.optimization_barrier(jnp.sum(weights, axis=1, keepdims=True))
        summed = jnp.dot(weights.astype(jnp.bfloat16), value_head, preferred_element_type=jnp.float32)
        return (summed / denominator).astype(jnp.bfloat16)
    heads_out = lax.map(one_head, (split_heads(queries), split_heads(keys), split_heads(values)))
    return heads_out.transpose(1, 0, 2).reshape(TOKENS, DIM)
```

```python
import functools
import math

import jax
import jax.numpy as jnp
from jax import lax
from jax.experimental import pallas as pl
from jax.experimental.pallas import tpu as pltpu
from jax.sharding import PartitionSpec as P

HEADS = 24
AXES = ("blk", "uly")
QUERY_TILE = 256


def attend_block(running, query_heads, key_piece, value_piece):
    running_max, running_sum, weighted = running
    score_scale = 1.0 / math.sqrt(query_heads.shape[2])
    scores = (
        jnp.einsum("hre,phe->hrp", query_heads, key_piece, preferred_element_type=jnp.float32)
        * score_scale
    )
    new_max = jnp.maximum(running_max, jnp.max(scores, axis=-1))
    factor = jnp.exp(running_max - new_max)
    weights = jnp.exp(scores - new_max[..., None])
    running_sum = running_sum * factor + jnp.sum(weights, axis=-1)
    product = jnp.einsum(
        "hrp,phe->hre",
        weights.astype(jnp.bfloat16),
        value_piece,
        preferred_element_type=jnp.float32,
    )
    weighted = weighted * factor[..., None] + product
    return (new_max, running_sum, weighted)


def make_folder(query_heads, running, pieces):
    head_count = query_heads.shape[0]
    head_width = query_heads.shape[2]
    key_piece = pieces[0].reshape(-1, head_count, head_width)
    value_piece = pieces[1].reshape(-1, head_count, head_width)
    length = key_piece.shape[0]
    if length > 1024 and length % 1024 == 0:
        key_stack = key_piece.reshape(length // 1024, 1024, head_count, head_width)
        value_stack = value_piece.reshape(length // 1024, 1024, head_count, head_width)

        def advance(state_now, blocks):
            return (attend_block(state_now, query_heads, blocks[0], blocks[1]), None)

        running, unused = lax.scan(advance, running, (key_stack, value_stack))
        return running
    return attend_block(running, query_heads, key_piece, value_piece)


def start_state(query_heads):
    head_count, block_rows, head_width = query_heads.shape
    lowest = jnp.full((head_count, block_rows), -jnp.inf, jnp.float32)
    return (
        lowest,
        jnp.zeros((head_count, block_rows), jnp.float32),
        jnp.zeros((head_count, block_rows, head_width), jnp.float32),
    )


def finish(running_sum, weighted):
    head_count, block_rows, head_width = weighted.shape
    normed = weighted / running_sum[..., None]
    return (
        normed.transpose(1, 0, 2).reshape(block_rows, head_count * head_width).astype(jnp.bfloat16)
    )


def local(queries, keys, values):
    groups = lax.axis_size("uly")
    heads_here = HEADS // groups
    head_width = queries.shape[1] // HEADS
    query_rows, key_rows, value_rows = (
        lax.all_to_all(queries, "uly", split_axis=1, concat_axis=0, tiled=True),
        lax.all_to_all(keys, "uly", split_axis=1, concat_axis=0, tiled=True),
        lax.all_to_all(values, "uly", split_axis=1, concat_axis=0, tiled=True),
    )
    block_rows = query_rows.shape[0]
    query_heads = query_rows.reshape(block_rows, heads_here, head_width).transpose(1, 0, 2)
    final_max, final_sum, weighted = make_folder(
        query_heads,
        start_state(query_heads),
        (
            lax.all_gather(key_rows, "blk", axis=0, tiled=True),
            lax.all_gather(value_rows, "blk", axis=0, tiled=True),
        ),
    )
    local_out = finish(final_sum, weighted)
    return lax.all_to_all(local_out, "uly", split_axis=0, concat_axis=1, tiled=True)


def head_kernel(tile, received, out):
    devices, rows, width = out.shape
    tokens = devices * rows
    factor = math.log2(math.e) / math.sqrt(width)
    key_rows = received[:, rows : 2 * rows, :].reshape(tokens, width)
    value_rows = received[:, 2 * rows :, :].reshape(tokens, width)
    step = tile // rows
    for first in range(0, devices, step):
        query_rows = received[first : first + step, :rows, :].reshape(tile, width)
        scores = lax.dot_general(
            query_rows, key_rows, (((1,), (1,)), ((), ())), preferred_element_type=jnp.float32
        )
        highest = jnp.max(scores, axis=1, keepdims=True)
        weights = jnp.exp2((scores - highest) * factor)
        denominator = jnp.sum(weights, axis=1, keepdims=True)
        summed = jnp.dot(
            weights.astype(jnp.bfloat16), value_rows, preferred_element_type=jnp.float32
        )
        attended = (summed / denominator).astype(jnp.bfloat16)
        out[first : first + step] = attended.reshape(step, rows, width)


def whole_heads(queries, keys, values):
    devices = lax.axis_size(AXES)
    rows, dim = queries.shape
    width = dim // HEADS
    packed = jnp.concatenate([queries, keys, values], axis=0).reshape(3 * rows, HEADS, width)
    packed = jnp.pad(packed.transpose(1, 0, 2), ((0, devices - HEADS), (0, 0), (0, 0)))
    received = lax.all_to_all(packed, AXES, split_axis=0, concat_axis=0, tiled=True)
    attended = pl.pallas_call(
        functools.partial(head_kernel, QUERY_TILE),
        out_shape=jax.ShapeDtypeStruct((devices, rows, width), jnp.bfloat16),
        compiler_params=pltpu.CompilerParams(vmem_limit_bytes=40 * 1024 * 1024),
    )(received)
    returned = lax.all_to_all(attended, AXES, split_axis=0, concat_axis=0, tiled=True)
    return returned[:HEADS].transpose(1, 0, 2).reshape(rows, dim)


def solution(mesh):
    in_specs = (P(AXES, None), P(AXES, None), P(AXES, None))
    out_specs = P(AXES, None)
    devices = mesh.shape["blk"] * mesh.shape["uly"]
    body = whole_heads if HEADS <= devices < 2 * HEADS else local
    return jax.shard_map(body, mesh=mesh, in_specs=in_specs, out_specs=out_specs, check_vma=False)
```

```python
import functools
import math

import jax
import jax.numpy as jnp
from jax import lax
from jax.experimental import pallas as pl
from jax.experimental.pallas import tpu as pltpu
from jax.sharding import PartitionSpec as P

HEADS = 24
AXES = ("blk", "uly")
QUERY_TILE = 256
STRIDE = 3


def attend_block(running, query_heads, key_piece, value_piece):
    running_max, running_sum, weighted = running
    score_scale = 1.0 / math.sqrt(query_heads.shape[2])
    scores = (
        jnp.einsum("hre,phe->hrp", query_heads, key_piece, preferred_element_type=jnp.float32)
        * score_scale
    )
    new_max = jnp.maximum(running_max, jnp.max(scores, axis=-1))
    factor = jnp.exp(running_max - new_max)
    weights = jnp.exp(scores - new_max[..., None])
    running_sum = running_sum * factor + jnp.sum(weights, axis=-1)
    product = jnp.einsum(
        "hrp,phe->hre",
        weights.astype(jnp.bfloat16),
        value_piece,
        preferred_element_type=jnp.float32,
    )
    weighted = weighted * factor[..., None] + product
    return (new_max, running_sum, weighted)


def make_folder(query_heads, running, pieces):
    head_count = query_heads.shape[0]
    head_width = query_heads.shape[2]
    key_piece = pieces[0].reshape(-1, head_count, head_width)
    value_piece = pieces[1].reshape(-1, head_count, head_width)
    length = key_piece.shape[0]
    if length > 1024 and length % 1024 == 0:
        key_stack = key_piece.reshape(length // 1024, 1024, head_count, head_width)
        value_stack = value_piece.reshape(length // 1024, 1024, head_count, head_width)

        def advance(state_now, blocks):
            return (attend_block(state_now, query_heads, blocks[0], blocks[1]), None)

        running, unused = lax.scan(advance, running, (key_stack, value_stack))
        return running
    return attend_block(running, query_heads, key_piece, value_piece)


def start_state(query_heads):
    head_count, block_rows, head_width = query_heads.shape
    lowest = jnp.full((head_count, block_rows), -jnp.inf, jnp.float32)
    return (
        lowest,
        jnp.zeros((head_count, block_rows), jnp.float32),
        jnp.zeros((head_count, block_rows, head_width), jnp.float32),
    )


def finish(running_sum, weighted):
    head_count, block_rows, head_width = weighted.shape
    normed = weighted / running_sum[..., None]
    return (
        normed.transpose(1, 0, 2).reshape(block_rows, head_count * head_width).astype(jnp.bfloat16)
    )


def local(queries, keys, values):
    groups = lax.axis_size("uly")
    heads_here = HEADS // groups
    head_width = queries.shape[1] // HEADS
    query_rows, key_rows, value_rows = (
        lax.all_to_all(queries, "uly", split_axis=1, concat_axis=0, tiled=True),
        lax.all_to_all(keys, "uly", split_axis=1, concat_axis=0, tiled=True),
        lax.all_to_all(values, "uly", split_axis=1, concat_axis=0, tiled=True),
    )
    block_rows = query_rows.shape[0]
    query_heads = query_rows.reshape(block_rows, heads_here, head_width).transpose(1, 0, 2)
    final_max, final_sum, weighted = make_folder(
        query_heads,
        start_state(query_heads),
        (
            lax.all_gather(key_rows, "blk", axis=0, tiled=True),
            lax.all_gather(value_rows, "blk", axis=0, tiled=True),
        ),
    )
    local_out = finish(final_sum, weighted)
    return lax.all_to_all(local_out, "uly", split_axis=0, concat_axis=1, tiled=True)


def participants(devices):
    return [STRIDE * i % devices for i in range(devices)]


def head_kernel(order, tile, received, out):
    devices, rows, width = out.shape
    tokens = devices * rows
    factor = math.log2(math.e) / math.sqrt(width)
    step = tile // rows
    me = lax.axis_index("blk") * lax.axis_size("uly") + lax.axis_index("uly")
    idle = functools.reduce(jnp.logical_or, [me == device for device in order[HEADS:]], False)

    def scores_of(first, key_rows):
        query_rows = received[first : first + step, :rows, :].reshape(tile, width)
        return lax.dot_general(
            query_rows, key_rows, (((1,), (1,)), ((), ())), preferred_element_type=jnp.float32
        )

    @pl.when(jnp.logical_not(idle))
    def attend():
        key_rows = received[:, rows : 2 * rows, :].reshape(tokens, width)
        value_rows = received[:, 2 * rows :, :].reshape(tokens, width)
        extended = jnp.concatenate([value_rows, jnp.ones_like(value_rows)], axis=1)
        scores = scores_of(0, key_rows)
        for first in range(0, devices, step):
            after = first + step
            later = scores_of(after, key_rows) if after < devices else None
            highest = jnp.max(scores, axis=1, keepdims=True)
            weights = jnp.exp2((scores - highest) * factor).astype(jnp.bfloat16)
            summed = jnp.dot(weights, extended, preferred_element_type=jnp.float32)
            attended = (summed[:, :width] / summed[:, width:]).astype(jnp.bfloat16)
            out[first:after] = attended.reshape(step, rows, width)
            scores = later


def whole_heads(queries, keys, values):
    devices = lax.axis_size(AXES)
    rows, dim = queries.shape
    width = dim // HEADS
    order = participants(devices)
    exchange = functools.partial(
        lax.all_to_all,
        axis_name=AXES,
        split_axis=0,
        concat_axis=0,
        axis_index_groups=[order],
        tiled=True,
    )
    packed = jnp.concatenate([queries, keys, values], axis=0).reshape(3 * rows, HEADS, width)
    packed = jnp.pad(packed.transpose(1, 0, 2), ((0, devices - HEADS), (0, 0), (0, 0)))
    attended = pl.pallas_call(
        functools.partial(head_kernel, order, min(QUERY_TILE, devices * rows)),
        out_shape=jax.ShapeDtypeStruct((devices, rows, width), jnp.bfloat16),
        compiler_params=pltpu.CompilerParams(vmem_limit_bytes=40 * 1024 * 1024),
    )(exchange(packed))
    returned = exchange(attended)
    return returned[:HEADS].transpose(1, 0, 2).reshape(rows, dim)


def solution(mesh):
    in_specs = (P(AXES, None), P(AXES, None), P(AXES, None))
    out_specs = P(AXES, None)
    devices = mesh.shape["blk"] * mesh.shape["uly"]
    body = whole_heads if HEADS <= devices < 2 * HEADS and devices % STRIDE else local
    return jax.shard_map(body, mesh=mesh, in_specs=in_specs, out_specs=out_specs, check_vma=False)
```

```python
import functools
import math

import jax
import jax.numpy as jnp
from jax import lax
from jax.experimental import pallas as pl
from jax.experimental.pallas import tpu as pltpu
from jax.sharding import PartitionSpec as P

HEADS = 24
AXES = ("blk", "uly")
QUERY_TILE = 256
STRIDE = 11
START = 19


def attend_block(running, query_heads, key_piece, value_piece):
    running_max, running_sum, weighted = running
    score_scale = 1.0 / math.sqrt(query_heads.shape[2])
    scores = (
        jnp.einsum("hre,phe->hrp", query_heads, key_piece, preferred_element_type=jnp.float32)
        * score_scale
    )
    new_max = jnp.maximum(running_max, jnp.max(scores, axis=-1))
    factor = jnp.exp(running_max - new_max)
    weights = jnp.exp(scores - new_max[..., None])
    running_sum = running_sum * factor + jnp.sum(weights, axis=-1)
    product = jnp.einsum(
        "hrp,phe->hre",
        weights.astype(jnp.bfloat16),
        value_piece,
        preferred_element_type=jnp.float32,
    )
    weighted = weighted * factor[..., None] + product
    return (new_max, running_sum, weighted)


def make_folder(query_heads, running, pieces):
    head_count = query_heads.shape[0]
    head_width = query_heads.shape[2]
    key_piece = pieces[0].reshape(-1, head_count, head_width)
    value_piece = pieces[1].reshape(-1, head_count, head_width)
    length = key_piece.shape[0]
    if length > 1024 and length % 1024 == 0:
        key_stack = key_piece.reshape(length // 1024, 1024, head_count, head_width)
        value_stack = value_piece.reshape(length // 1024, 1024, head_count, head_width)

        def advance(state_now, blocks):
            return (attend_block(state_now, query_heads, blocks[0], blocks[1]), None)

        running, unused = lax.scan(advance, running, (key_stack, value_stack))
        return running
    return attend_block(running, query_heads, key_piece, value_piece)


def start_state(query_heads):
    head_count, block_rows, head_width = query_heads.shape
    lowest = jnp.full((head_count, block_rows), -jnp.inf, jnp.float32)
    return (
        lowest,
        jnp.zeros((head_count, block_rows), jnp.float32),
        jnp.zeros((head_count, block_rows, head_width), jnp.float32),
    )


def finish(running_sum, weighted):
    head_count, block_rows, head_width = weighted.shape
    normed = weighted / running_sum[..., None]
    return (
        normed.transpose(1, 0, 2).reshape(block_rows, head_count * head_width).astype(jnp.bfloat16)
    )


def local(queries, keys, values):
    groups = lax.axis_size("uly")
    heads_here = HEADS // groups
    head_width = queries.shape[1] // HEADS
    query_rows, key_rows, value_rows = (
        lax.all_to_all(queries, "uly", split_axis=1, concat_axis=0, tiled=True),
        lax.all_to_all(keys, "uly", split_axis=1, concat_axis=0, tiled=True),
        lax.all_to_all(values, "uly", split_axis=1, concat_axis=0, tiled=True),
    )
    block_rows = query_rows.shape[0]
    query_heads = query_rows.reshape(block_rows, heads_here, head_width).transpose(1, 0, 2)
    final_max, final_sum, weighted = make_folder(
        query_heads,
        start_state(query_heads),
        (
            lax.all_gather(key_rows, "blk", axis=0, tiled=True),
            lax.all_gather(value_rows, "blk", axis=0, tiled=True),
        ),
    )
    local_out = finish(final_sum, weighted)
    return lax.all_to_all(local_out, "uly", split_axis=0, concat_axis=1, tiled=True)


def participants(blocks, groups):
    devices = blocks * groups
    if blocks % 4 or math.gcd(STRIDE, devices) > 1:
        return list(range(devices))
    order = []
    for place in range(devices):
        pair, rest = divmod((STRIDE * place + START) % devices, 2 * groups)
        group, half = divmod(rest, 2)
        order.append(((pair ^ 1) * 2 + (half ^ 1)) * groups + group)
    return order


def head_kernel(order, tile, received, out):
    devices, rows, width = out.shape
    tokens = devices * rows
    factor = math.log2(math.e) / math.sqrt(width)
    step = tile // rows
    me = lax.axis_index("blk") * lax.axis_size("uly") + lax.axis_index("uly")
    idle = functools.reduce(jnp.logical_or, [me == device for device in order[HEADS:]], False)

    def scores_of(first, key_rows):
        query_rows = received[first : first + step, :rows, :].reshape(tile, width)
        return lax.dot_general(
            query_rows, key_rows, (((1,), (1,)), ((), ())), preferred_element_type=jnp.float32
        )

    @pl.when(jnp.logical_not(idle))
    def attend():
        key_rows = received[:, rows : 2 * rows, :].reshape(tokens, width)
        value_rows = received[:, 2 * rows :, :].reshape(tokens, width)
        extended = jnp.concatenate([value_rows, jnp.ones_like(value_rows)], axis=1)
        scores = scores_of(0, key_rows)
        for first in range(0, devices, step):
            after = first + step
            later = scores_of(after, key_rows) if after < devices else None
            highest = jnp.max(scores, axis=1, keepdims=True)
            weights = jnp.exp2((scores - highest) * factor).astype(jnp.bfloat16)
            summed = jnp.dot(weights, extended, preferred_element_type=jnp.float32)
            attended = (summed[:, :width] / summed[:, width:]).astype(jnp.bfloat16)
            out[first:after] = attended.reshape(step, rows, width)
            scores = later


def whole_heads(queries, keys, values):
    devices = lax.axis_size(AXES)
    rows, dim = queries.shape
    width = dim // HEADS
    order = participants(lax.axis_size("blk"), lax.axis_size("uly"))
    exchange = functools.partial(
        lax.all_to_all,
        axis_name=AXES,
        split_axis=0,
        concat_axis=0,
        axis_index_groups=[order],
        tiled=True,
    )
    packed = jnp.concatenate([queries, keys, values], axis=0).reshape(3 * rows, HEADS, width)
    packed = jnp.pad(packed.transpose(1, 0, 2), ((0, devices - HEADS), (0, 0), (0, 0)))
    attended = pl.pallas_call(
        functools.partial(head_kernel, order, min(QUERY_TILE, devices * rows)),
        out_shape=jax.ShapeDtypeStruct((devices, rows, width), jnp.bfloat16),
        compiler_params=pltpu.CompilerParams(vmem_limit_bytes=40 * 1024 * 1024),
    )(exchange(packed))
    returned = exchange(attended)
    return returned[:HEADS].transpose(1, 0, 2).reshape(rows, dim)


def solution(mesh):
    in_specs = (P(AXES, None), P(AXES, None), P(AXES, None))
    out_specs = P(AXES, None)
    devices = mesh.shape["blk"] * mesh.shape["uly"]
    body = whole_heads if HEADS <= devices < 2 * HEADS else local
    return jax.shard_map(body, mesh=mesh, in_specs=in_specs, out_specs=out_specs, check_vma=False)
```

```python
import functools
import math

import jax
import jax.numpy as jnp
from jax import lax
from jax.experimental import pallas as pl
from jax.experimental.pallas import tpu as pltpu
from jax.sharding import PartitionSpec as P

HEADS = 24
AXES = ("blk", "uly")
QUERY_TILE = 256
STRIDE = 11
START = 19


def attend_block(running, query_heads, key_piece, value_piece):
    running_max, running_sum, weighted = running
    score_scale = 1.0 / math.sqrt(query_heads.shape[2])
    scores = (
        jnp.einsum("hre,phe->hrp", query_heads, key_piece, preferred_element_type=jnp.float32)
        * score_scale
    )
    new_max = jnp.maximum(running_max, jnp.max(scores, axis=-1))
    factor = jnp.exp(running_max - new_max)
    weights = jnp.exp(scores - new_max[..., None])
    running_sum = running_sum * factor + jnp.sum(weights, axis=-1)
    product = jnp.einsum(
        "hrp,phe->hre",
        weights.astype(jnp.bfloat16),
        value_piece,
        preferred_element_type=jnp.float32,
    )
    weighted = weighted * factor[..., None] + product
    return (new_max, running_sum, weighted)


def make_folder(query_heads, running, pieces):
    head_count = query_heads.shape[0]
    head_width = query_heads.shape[2]
    key_piece = pieces[0].reshape(-1, head_count, head_width)
    value_piece = pieces[1].reshape(-1, head_count, head_width)
    length = key_piece.shape[0]
    if length > 1024 and length % 1024 == 0:
        key_stack = key_piece.reshape(length // 1024, 1024, head_count, head_width)
        value_stack = value_piece.reshape(length // 1024, 1024, head_count, head_width)

        def advance(state_now, blocks):
            return (attend_block(state_now, query_heads, blocks[0], blocks[1]), None)

        running, unused = lax.scan(advance, running, (key_stack, value_stack))
        return running
    return attend_block(running, query_heads, key_piece, value_piece)


def start_state(query_heads):
    head_count, block_rows, head_width = query_heads.shape
    lowest = jnp.full((head_count, block_rows), -jnp.inf, jnp.float32)
    return (
        lowest,
        jnp.zeros((head_count, block_rows), jnp.float32),
        jnp.zeros((head_count, block_rows, head_width), jnp.float32),
    )


def finish(running_sum, weighted):
    head_count, block_rows, head_width = weighted.shape
    normed = weighted / running_sum[..., None]
    return (
        normed.transpose(1, 0, 2).reshape(block_rows, head_count * head_width).astype(jnp.bfloat16)
    )


def local(queries, keys, values):
    groups = lax.axis_size("uly")
    heads_here = HEADS // groups
    head_width = queries.shape[1] // HEADS
    query_rows, key_rows, value_rows = (
        lax.all_to_all(queries, "uly", split_axis=1, concat_axis=0, tiled=True),
        lax.all_to_all(keys, "uly", split_axis=1, concat_axis=0, tiled=True),
        lax.all_to_all(values, "uly", split_axis=1, concat_axis=0, tiled=True),
    )
    block_rows = query_rows.shape[0]
    query_heads = query_rows.reshape(block_rows, heads_here, head_width).transpose(1, 0, 2)
    final_max, final_sum, weighted = make_folder(
        query_heads,
        start_state(query_heads),
        (
            lax.all_gather(key_rows, "blk", axis=0, tiled=True),
            lax.all_gather(value_rows, "blk", axis=0, tiled=True),
        ),
    )
    local_out = finish(final_sum, weighted)
    return lax.all_to_all(local_out, "uly", split_axis=0, concat_axis=1, tiled=True)


def participants(blocks, groups):
    devices = blocks * groups
    if blocks % 4 or math.gcd(STRIDE, devices) > 1:
        return list(range(devices))
    order = []
    for place in range(devices):
        pair, rest = divmod((STRIDE * place + START) % devices, 2 * groups)
        group, half = divmod(rest, 2)
        order.append(((pair ^ 1) * 2 + (half ^ 1)) * groups + group)
    return order


def head_kernel(order, tile, received, out):
    devices, rows, width = out.shape
    tokens = devices * rows
    factor = math.log2(math.e) / math.sqrt(width)
    step = tile // rows
    me = lax.axis_index("blk") * lax.axis_size("uly") + lax.axis_index("uly")
    idle = functools.reduce(jnp.logical_or, [me == device for device in order[HEADS:]], False)

    def scores_of(first, key_rows):
        query_rows = received[first : first + step, :rows, :].reshape(tile, width)
        return lax.dot_general(
            query_rows, key_rows, (((1,), (1,)), ((), ())), preferred_element_type=jnp.float32
        )

    @pl.when(jnp.logical_not(idle))
    def attend():
        key_rows = received[:, rows : 2 * rows, :].reshape(tokens, width)
        value_rows = received[:, 2 * rows :, :].reshape(tokens, width)
        scores = scores_of(0, key_rows)
        for first in range(0, devices, step):
            after = first + step
            later = scores_of(after, key_rows) if after < devices else None
            highest = jnp.max(scores, axis=1, keepdims=True)
            weights = jnp.exp2((scores - highest) * factor)
            denominator = jnp.sum(weights, axis=1, keepdims=True)
            summed = jnp.dot(
                weights.astype(jnp.bfloat16), value_rows, preferred_element_type=jnp.float32
            )
            attended = (summed / denominator).astype(jnp.bfloat16)
            out[first:after] = attended.reshape(step, rows, width)
            scores = later


def whole_heads(queries, keys, values):
    devices = lax.axis_size(AXES)
    rows, dim = queries.shape
    width = dim // HEADS
    order = participants(lax.axis_size("blk"), lax.axis_size("uly"))
    exchange = functools.partial(
        lax.all_to_all,
        axis_name=AXES,
        split_axis=0,
        concat_axis=0,
        axis_index_groups=[order],
        tiled=True,
    )
    packed = jnp.concatenate([queries, keys, values], axis=0).reshape(3 * rows, HEADS, width)
    packed = jnp.pad(packed.transpose(1, 0, 2), ((0, devices - HEADS), (0, 0), (0, 0)))
    attended = pl.pallas_call(
        functools.partial(head_kernel, order, min(QUERY_TILE, devices * rows)),
        out_shape=jax.ShapeDtypeStruct((devices, rows, width), jnp.bfloat16),
        compiler_params=pltpu.CompilerParams(vmem_limit_bytes=40 * 1024 * 1024),
    )(exchange(packed))
    returned = exchange(attended)
    return returned[:HEADS].transpose(1, 0, 2).reshape(rows, dim)


def solution(mesh):
    in_specs = (P(AXES, None), P(AXES, None), P(AXES, None))
    out_specs = P(AXES, None)
    devices = mesh.shape["blk"] * mesh.shape["uly"]
    body = whole_heads if HEADS <= devices < 2 * HEADS else local
    return jax.shard_map(body, mesh=mesh, in_specs=in_specs, out_specs=out_specs, check_vma=False)
```
